32 devices in a mesh: groups: 2 (over y), latent: 4 (over z), rows: 4 (over x, core).
Axes of the slice: x: 2, y: 2, z: 4, core: 2. Of those that a mesh axis runs over, the one named last changes fastest.
Arguments:
- activations_in: bfloat16 [2, 128, 2304], P('groups', None, 'latent'), parts along dimension 0, may hold values from -6 to 6
- gate_proj: bfloat16 [2304, 4608], P('rows', 'latent'), may hold values from -0.125 to 0.125
- up_proj: bfloat16 [2304, 4608], P('rows', 'latent'), may hold values from -0.125 to 0.125
- down_proj: bfloat16 [4608, 2304], P('latent', 'rows'), may hold values from -0.09375 to 0.09375
- enc_weight: bfloat16 [4608, 65536], P(('groups', 'rows'), 'latent'), parts along dimension 0, may hold values from -6 to 6
- enc_bias: float32 [131072], P(('groups', 'latent')), parts along dimension 0, may hold values from -0.5 to 0.5
- dec_weight: bfloat16 [131072, 2304], P(('groups', 'latent'), 'rows'), parts along dimension 0, may hold values from -6 to 6
- dec_bias: float32 [4608], P(('groups', 'rows')), parts along dimension 0, may hold values from -0.5 to 0.5
Outputs:
- enc_weight_new: bfloat16 [4608, 65536], P(('groups', 'rows'), 'latent'), parts along dimension 0
- enc_bias_new: float32 [131072], P(('groups', 'latent')), parts along dimension 0
- dec_weight_new: bfloat16 [131072, 2304], P(('groups', 'latent'), 'rows'), parts along dimension 0
- dec_bias_new: float32 [4608], P(('groups', 'rows')), parts along dimension 0
The draws below stay inside these ranges and needn't reach their ends.
There are 2 independent parts, one for each index of `groups`. The reference program is written for one: setup_inputs(seed, part) draws one part's arguments, and reference() takes and returns one part's arrays. A program takes and returns all parts, laid end to end along the dimension named above; an argument that names none is the same for every part. Nothing has to cross between parts.
All inputs are finite; a program needn't handle non-finite values.
Results may differ from the reference program's by a relative error of at most 0.02.
Values may be sent and summed in bfloat16 or wider, within the bound.
No kernel may reach another device: no remote copies, remote signals or barrier semaphores. Data moves between devices by JAX's collectives and lax.ppermute only.
A program may use at most 128 MiB of HBM per device.

```python
import jax
import jax.numpy as jnp
from jax import lax

MODEL_WIDTH = 2304
HIDDEN_UNITS = 4608
LATENTS = 65536
MINIBATCHES = 1
BATCH_TOKENS = 128
N_ROWS = 4


def level_of(rng, extent, shards, least, top_value):
    def one(dim, shards_of):
        heights = jax.random.uniform(jax.random.fold_in(jax.random.fold_in(rng, 6), dim), (shards_of,), jnp.float32, least / len(shards), top_value / len(shards))
        return jnp.repeat(jnp.exp(heights), extent[dim] // shards_of).reshape((-1,) + (1,) * (len(extent) - dim - 1))

    loudness = one(*shards[0])
    for cut in shards[1:]:
        loudness = loudness * one(*cut)
    return loudness


def noise(stream_key, extent, deviation, bound, cuts=(), dtype=jnp.bfloat16):
    result = jax.random.normal(stream_key, extent, jnp.float32) * deviation
    if len(cuts) > 0:
        result = level_of(stream_key, extent, cuts, -0.22, 0.18) * result
    return jnp.clip(result, min=-bound, max=bound).astype(dtype)


def setup_inputs(seed: int = 0, part: int = 0) -> dict:
    key_list = jax.random.split(jax.random.key(seed), 9)
    own_keys = jax.random.split(jax.random.fold_in(key_list[8], part), 9)
    return {
        "activations_in": noise(own_keys[0], (MINIBATCHES, BATCH_TOKENS, MODEL_WIDTH), 1.0, 6.0, ((2, 4),)),
        "gate_proj": noise(key_list[1], (MODEL_WIDTH, HIDDEN_UNITS), MODEL_WIDTH ** -0.5, 0.125, ((0, 4), (1, 4))),
        "up_proj": noise(key_list[2], (MODEL_WIDTH, HIDDEN_UNITS), MODEL_WIDTH ** -0.5, 0.125, ((0, 4), (1, 4))),
        "down_proj": noise(key_list[3], (HIDDEN_UNITS, MODEL_WIDTH), HIDDEN_UNITS ** -0.5, 0.09375, ((0, 4), (1, 4))),
        "enc_weight": noise(own_keys[4], (MODEL_WIDTH, LATENTS), 1.0, 6.0, ((0, 4), (1, 4))),
        "enc_bias": jnp.clip(jax.random.uniform(own_keys[5], (LATENTS,), jnp.float32, -0.5, 0.5) * level_of(own_keys[5], (LATENTS,), ((0, 4),), -0.4, 0.0), -0.5, 0.5),
        "dec_weight": noise(own_keys[6], (LATENTS, MODEL_WIDTH), 1.0, 6.0, ((0, 4), (1, 4))),
        "dec_bias": jnp.clip(jax.random.uniform(own_keys[7], (MODEL_WIDTH,), jnp.float32, -0.5, 0.5) * level_of(own_keys[7], (MODEL_WIDTH,), ((0, 4),), -0.4, 0.0), -0.5, 0.5),
    }


sparsity_cost = 0.1
sharpness = 8.0
weight_rate = 2.0
enc_bias_rate = 0.01
dec_bias_rate = 0.002


def smooth_relu(values):
    return jax.nn.softplus(sharpness * values) / sharpness


def reference(activations_in, gate_proj, up_proj, down_proj, enc_weight, enc_bias, dec_weight, dec_bias):
    flattened = activations_in.reshape(MINIBATCHES * BATCH_TOKENS, MODEL_WIDTH)
    gate_term = jnp.dot(flattened, gate_proj, preferred_element_type=jnp.float32)
    up_term = jnp.dot(flattened, up_proj, preferred_element_type=jnp.float32)
    hidden = (jax.nn.gelu(gate_term, approximate=True) * up_term).astype(jnp.bfloat16)
    features = jnp.dot(hidden, down_proj, preferred_element_type=jnp.float32).astype(jnp.bfloat16)
    features = features.reshape(MINIBATCHES, BATCH_TOKENS, MODEL_WIDTH)
    block_size = MODEL_WIDTH // N_ROWS
    enc_scale = MODEL_WIDTH ** -0.5
    dec_scale = LATENTS ** -0.5
    for batch_index in range(MINIBATCHES):
        inputs = features[batch_index]
        encoded = jnp.zeros((BATCH_TOKENS, LATENTS), jnp.float32)
        back_sum = jnp.zeros((BATCH_TOKENS, LATENTS), jnp.float32)
        for row_index in range(N_ROWS):
            lower = row_index * block_size
            term = jnp.dot(inputs[:, lower:lower + block_size], enc_weight[lower:lower + block_size],
                           preferred_element_type=jnp.float32).astype(jnp.bfloat16)
            encoded = encoded + lax.optimization_barrier(term).astype(jnp.float32)
        pre_latent = enc_scale * encoded + enc_bias
        latents = smooth_relu(pre_latent).astype(jnp.bfloat16)
        rebuilt = dec_scale * jnp.dot(latents, dec_weight, preferred_element_type=jnp.float32) + dec_bias
        residual_grad = (2.0 * (rebuilt - inputs.astype(jnp.float32))).astype(jnp.bfloat16)
        for row_index in range(N_ROWS):
            lower = row_index * block_size
            term = lax.dot_general(residual_grad[:, lower:lower + block_size], dec_weight[:, lower:lower + block_size],
                                   (((1,), (1,)), ((), ())), preferred_element_type=jnp.float32).astype(jnp.bfloat16)
            back_sum = back_sum + lax.optimization_barrier(term).astype(jnp.float32)
        latent_grad = (jax.nn.sigmoid(sharpness * pre_latent) * (dec_scale * back_sum + sparsity_cost)).astype(jnp.bfloat16)
        dec_grad = dec_scale * lax.dot_general(latents, residual_grad, (((0,), (0,)), ((), ())),
                                               preferred_element_type=jnp.float32)
        enc_grad = enc_scale * lax.dot_general(inputs, latent_grad, (((0,), (0,)), ((), ())),
                                               preferred_element_type=jnp.float32)
        enc_bias = enc_bias - enc_bias_rate * jnp.sum(latent_grad.astype(jnp.float32), axis=0)
        dec_bias = dec_bias - dec_bias_rate * jnp.sum(residual_grad.astype(jnp.float32), axis=0)
        enc_weight = (enc_weight.astype(jnp.float32) - weight_rate * enc_grad).astype(jnp.bfloat16)
        dec_weight = (dec_weight.astype(jnp.float32) - weight_rate * dec_grad).astype(jnp.bfloat16)
    return enc_weight, enc_bias, dec_weight, dec_bias
```

```python
import math

import jax
import jax.numpy as jnp
from jax import lax
from jax.experimental import pallas as pl
from jax.experimental.pallas import tpu as pltpu
from jax.sharding import PartitionSpec as P

sparsity_cost = 0.1
sharpness = 8.0
weight_rate = 2.0
enc_bias_rate = 0.01
dec_bias_rate = 0.002

BF16, F32 = jnp.bfloat16, jnp.float32
MIB = 2 ** 20
IN_VMEM = pl.BlockSpec(memory_space=pltpu.VMEM)
UNTOUCHED = pl.BlockSpec(memory_space=pl.ANY)


def dot(a, b, over):
    return lax.dot_general(a, b, (over, ((), ())), preferred_element_type=F32)


def flip(value, axis, size, bit):
    return lax.ppermute(value, axis, [(i, i ^ bit) for i in range(size)])


SENT_PARTS = 4


def stacked(refs):
    return jnp.concatenate([ref[...] for ref in refs], axis=0)


def spread(value, refs):
    rows = refs[0].shape[0]
    for i, ref in enumerate(refs):
        ref[...] = value[i * rows:(i + 1) * rows]


class Cut:
    def __init__(self, half, start, width):
        self.half, self.start, self.width = half, start, width
        self.step = math.gcd(math.gcd(half, start), math.gcd(width, 4096))
        while self.step > 2048:
            self.step //= 2
        self.steps = width // self.step
        self.grid = 2 * self.steps

    def first(self, rows):
        return pl.BlockSpec((rows, self.step), lambda j, side: (0, jnp.minimum(j, self.steps - 1)))

    def second(self, rows):
        return pl.BlockSpec((rows, self.step), lambda j, side: (0, jnp.maximum(j - self.steps, 0)))

    def place(self, j, side):
        late = jnp.where(j < self.steps, 0, 1)
        half = jnp.where(j < self.steps, 1 - side[0], side[0])
        return (half * self.half + self.start) // self.step + j - late * self.steps

    def whole(self, rows):
        return pl.BlockSpec((rows, self.step), lambda j, side: (0, self.place(j, side)))

    def columns(self, side):
        return pl.ds(pl.multiple_of(self.place(pl.program_id(0), side) * self.step, self.step), self.step)

    def pick(self, first_refs, second_ref):
        return jnp.where(pl.program_id(0) < self.steps, stacked(first_refs), second_ref[...])


def cuts_of(half, shares):
    unit = half // sum(shares)
    if unit * sum(shares) != half or unit % 128:
        return [Cut(half, 0, half)]
    cuts, start = [], 0
    for share in shares:
        cuts.append(Cut(half, start, share * unit))
        start += share * unit
    return cuts


def shape(*dims, dtype=BF16):
    return jax.ShapeDtypeStruct(dims, dtype)


class Order:
    def __init__(self, side):
        self.side = side
        self.thread = jnp.zeros((8, 128), F32)
        self.kept = {}

    def call(self, kernel, grid, operands, in_specs, out_specs, out_shape, use=(), aliases=None, vmem=6, scratch=(),
             bring=None):
        names, bring = list(self.kept), bring or {}
        n_in, n_out, n_kept, n_new = len(operands), len(out_shape), len(names), len(bring)
        pieces = 12

        def within(side_ref, *refs):
            ins, refs = refs[:n_in], refs[n_in:]
            weights, refs = dict(zip(names, refs[:n_kept])), refs[n_kept + 1:]
            sources, refs = refs[:n_new], refs[n_new:]
            outs, refs = refs[:n_out], refs[n_out + n_kept + 1:]
            targets, refs = refs[:n_new], refs[n_new:]
            copies = []
            for source, target in zip(sources, targets):
                count = math.gcd(source.shape[0] // 16, pieces)
                rows = source.shape[0] // count
                for i in range(count):
                    part = pl.ds(i * rows, rows)
                    copies.append(pltpu.make_async_copy(source.at[part], target.at[part], refs[-1].at[len(copies)]))
            step = pl.program_id(0)

            @pl.when(step == 0)
            def _():
                for copy in copies:
                    copy.start()

            kernel(side_ref, *ins, *[weights[name] for name in use], *outs, *(refs[:-1] if bring else refs))

            @pl.when(step == grid - 1)
            def _():
                for copy in copies:
                    copy.wait()

        kept = [pltpu.with_memory_space_constraint(self.kept[name], pltpu.VMEM) for name in names]
        new = [pltpu.with_memory_space_constraint(weight, pltpu.HBM) for weight in bring.values()]
        joined = dict(aliases or {})
        joined.update({1 + n_in + i: n_out + i for i in range(n_kept + 1)})
        results = pl.pallas_call(
            within,
            grid_spec=pltpu.PrefetchScalarGridSpec(
                num_scalar_prefetch=1,
                grid=(grid,),
                in_specs=in_specs + [IN_VMEM] * n_kept + [UNTOUCHED] + [pl.BlockSpec(memory_space=pltpu.HBM)] * n_new,
                out_specs=out_specs + [IN_VMEM] * n_kept + [UNTOUCHED] + [IN_VMEM] * n_new,
                scratch_shapes=list(scratch) + ([pltpu.SemaphoreType.DMA((pieces * n_new,))] if bring else []),
            ),
            out_shape=out_shape
            + [pltpu.VMEM(k.shape, k.dtype) for k in kept]
            + [shape(8, 128, dtype=F32)]
            + [pltpu.VMEM(w.shape, w.dtype) for w in new],
            input_output_aliases=joined,
            compiler_params=pltpu.CompilerParams(vmem_limit_bytes=vmem * MIB),
            cost_estimate=pl.CostEstimate(flops=1, bytes_accessed=1, transcendentals=0),
        )(self.side, *operands, *kept, self.thread, *new)
        self.kept = dict(zip(names, results[n_out:]))
        self.thread = results[n_out + n_kept]
        self.kept.update(zip(bring, results[n_out + n_kept + 1:]))
        return list(results[:n_out])

    def keep(self, **weights):
        self.call(lambda *refs: None, 1, (), [], [], [], vmem=1, bring=weights)

    def drop(self, *names):
        for name in names:
            del self.kept[name]


def project(run, cut, tokens, weight):
    count, width = tokens.shape

    def kernel(side_ref, tokens_ref, weight_ref, *refs):
        product = dot(tokens_ref[...], weight_ref[:, cut.columns(side_ref)], ((1,), (0,))).astype(BF16)
        late = pl.program_id(0) >= cut.steps

        @pl.when(jnp.logical_not(late))
        def _():
            spread(product, refs[:-1])

        @pl.when(late)
        def _():
            refs[-1][...] = product

    each = count // SENT_PARTS
    *for_other, mine = run.call(
        kernel, cut.grid, (tokens,), [IN_VMEM], [cut.first(each)] * SENT_PARTS + [cut.second(count)],
        [shape(each, cut.width)] * SENT_PARTS + [shape(count, cut.width)], use=[weight],
    )
    return for_other, mine


def added(run, mine, received, dtype=BF16):
    def kernel(side_ref, mine_ref, received_ref, out_ref):
        out_ref[...] = (mine_ref[...].astype(F32) + received_ref[...].astype(F32)).astype(dtype)

    return run.call(
        kernel, 1, (mine, received), [IN_VMEM] * 2, [IN_VMEM], [shape(*mine.shape, dtype=dtype)],
    )[0]


def added_parts(run, mine, received):
    def kernel(side_ref, mine_ref, *refs):
        refs[-1][...] = (mine_ref[...].astype(F32) + stacked(refs[:-1]).astype(F32)).astype(BF16)

    return run.call(
        kernel, 1, (mine, *received), [IN_VMEM] * (1 + len(received)), [IN_VMEM], [shape(*mine.shape)]
    )[0]


def token_parts(run, activations_t, parts, rows):
    width, count = activations_t.shape
    each = count // parts

    def kernel(side_ref, activations_ref, *refs):
        tokens = activations_ref[...].T
        for part, out_ref in enumerate(refs[len(rows):len(rows) + parts]):
            out_ref[...] = tokens[part * each:(part + 1) * each]

    results = run.call(
        kernel, 1, (activations_t,) + tuple(rows), [IN_VMEM] + [UNTOUCHED] * len(rows),
        [IN_VMEM] * parts + [UNTOUCHED] * len(rows),
        [shape(each, width)] * parts + [shape(*r.shape, dtype=r.dtype) for r in rows],
        aliases={2 + i: parts + i for i in range(len(rows))},
    )
    return results[:parts], results[parts:]


def turned(run, parts):
    count, width = parts[0].shape

    def kernel(side_ref, first_ref, second_ref, out_ref):
        out_ref[...] = jnp.concatenate([first_ref[...], second_ref[...]], axis=0).T

    return run.call(
        kernel, 1, tuple(parts), [IN_VMEM] * 2, [IN_VMEM], [shape(width, 2 * count)]
    )[0]


def residual_grad(run, mine, received, bias, features, dec_scale):
    def kernel(side_ref, mine_ref, received_ref, bias_ref, features_ref, out_ref):
        rebuilt = dec_scale * (mine_ref[...].astype(F32) + received_ref[...].astype(F32)) + bias_ref[...]
        out_ref[...] = (2.0 * (rebuilt - features_ref[...].astype(F32))).astype(BF16)

    return run.call(
        kernel, 1, (mine, received, bias, features), [IN_VMEM] * 4, [IN_VMEM], [shape(*features.shape)],
    )[0]


def update_bias(run, bias, parts):
    def kernel(side_ref, bias_ref, first_ref, second_ref, out_ref):
        both = jnp.concatenate([first_ref[...], second_ref[...]], axis=0).astype(F32)
        out_ref[...] = (bias_ref[...] - dec_bias_rate * jnp.sum(both, axis=0, keepdims=True)).reshape(out_ref.shape)

    return run.call(
        kernel, 1, (bias,) + tuple(parts), [IN_VMEM] * 3, [IN_VMEM], [shape(bias.shape[1], dtype=F32)],
    )[0]


def gate_or_up(run, own, tokens, hidden, received=None):
    count = tokens.shape[0]

    def kernel(side_ref, tokens_ref, *refs):
        gate_ref, up_ref, out_ref = refs[-3:]
        for value, weight_ref in enumerate((gate_ref, up_ref) if own else (up_ref, gate_ref)):
            @pl.when(side_ref[0] == value)
            def _():
                total = dot(tokens_ref[...], weight_ref[...], ((1,), (0,)))
                if received is not None:
                    total = total + refs[0][...].astype(F32)
                out_ref[...] = total.astype(BF16)

    more = () if received is None else (received,)
    return run.call(
        kernel, 1, (tokens,) + more, [IN_VMEM] * (1 + len(more)), [IN_VMEM], [shape(count, hidden)],
        use=["gate", "up"],
    )[0]


def layer_output(run, own_term, other_term, width):
    count, hidden = own_term.shape

    def kernel(side_ref, own_ref, other_ref, down_ref, out_ref):
        for value, (gate_ref, up_ref) in enumerate(((own_ref, other_ref), (other_ref, own_ref))):
            @pl.when(side_ref[0] == value)
            def _():
                hidden = (jax.nn.gelu(gate_ref[...], approximate=True) * up_ref[...]).astype(BF16)
                out_ref[...] = dot(hidden, down_ref[...], ((1,), (1,))).astype(BF16)

    return run.call(
        kernel, 1, (own_term, other_term), [IN_VMEM] * 2, [IN_VMEM], [shape(count, width)], use=["down"],
    )[0]


def pre_of(mine, other, bias, enc_scale):
    return enc_scale * (mine.astype(F32) + other.astype(F32)) + bias


def over_own(cut):
    def local(rows):
        return pl.BlockSpec((rows, cut.step), lambda j, side: (0, j))

    def whole(rows):
        return pl.BlockSpec((rows, cut.step), lambda j, side: (0, cut.place(j + cut.steps, side)))

    return local, whole


def latents_of(run, cut, mine, other, bias, enc_scale):
    count = mine.shape[0]
    local, whole = over_own(cut)

    def kernel(side_ref, mine_ref, other_ref, bias_ref, latents_ref, *sent_refs):
        scaled = sharpness * pre_of(mine_ref[...], other_ref[...], bias_ref[...], enc_scale)
        soft = jnp.maximum(scaled, 0.0) + jnp.log1p(jnp.exp(-jnp.abs(scaled)))
        latents = (soft * (1.0 / sharpness)).astype(BF16)
        latents_ref[...] = latents
        spread(latents, sent_refs)

    each = count // SENT_PARTS
    latents, *sent = run.call(
        kernel, cut.steps, (mine, other, bias), [local(count), local(count), whole(1)],
        [local(count)] + [local(each)] * SENT_PARTS,
        [shape(count, cut.width)] + [shape(each, cut.width)] * SENT_PARTS,
    )
    return latents, sent


def decode(run, cut, latents_other, latents_own, weight, width, partial, last):
    count = latents_own.shape[0]

    n_first = len(latents_other)

    def kernel(side_ref, *refs):
        first_refs, second_ref = refs[:n_first], refs[n_first]
        weight_ref, sum_ref, total = refs[-3:]

        @pl.when(pl.program_id(0) == 0)
        def _():
            total[...] = jnp.zeros_like(total) if partial is None else refs[n_first + 1][...]

        total[...] += dot(
            cut.pick(first_refs, second_ref), weight_ref[:, cut.columns(side_ref)], ((1,), (1,))
        )

        @pl.when(pl.program_id(0) == cut.grid - 1)
        def _():
            sum_ref[...] = total[...].astype(sum_ref.dtype)

    more = () if partial is None else (partial,)
    return run.call(
        kernel, cut.grid, (*latents_other, latents_own) + more,
        [cut.first(count // n_first)] * n_first + [cut.second(count)] + [IN_VMEM] * len(more),
        [pl.BlockSpec((count, width), lambda j, side: (0, 0))],
        [shape(count, width, dtype=BF16 if last else F32)],
        use=[weight], scratch=[pltpu.VMEM((count, width), F32)],
    )[0]


def latent_grad(run, cut, mine, other, bias, back, back_other, enc_scale, dec_scale):
    count = mine.shape[0]
    local, whole = over_own(cut)

    def kernel(side_ref, mine_ref, other_ref, bias_ref, back_ref, back_other_ref, grad_ref, *sent_refs):
        scaled = sharpness * pre_of(mine_ref[...], other_ref[...], bias_ref[...], enc_scale)
        total = back_ref[...].astype(F32) + back_other_ref[...].astype(F32)
        grad = (jax.nn.sigmoid(scaled) * (dec_scale * total + sparsity_cost)).astype(BF16)
        grad_ref[...] = grad
        spread(grad, sent_refs)

    each = count // SENT_PARTS
    grad, *sent = run.call(
        kernel, cut.steps, (mine, other, bias, back, back_other),
        [local(count), local(count), whole(1), local(count), local(count)],
        [local(count)] + [local(each)] * SENT_PARTS,
        [shape(count, cut.width)] + [shape(each, cut.width)] * SENT_PARTS,
    )
    return grad, sent


def update(run, cut, left, rights, weight, scale, target, latents, bias=None):
    width = left.shape[0]
    count, n_first = rights[0][1].shape[0], len(rights[0][0])
    each = n_first + 1
    given = () if bias is None else (bias,)
    more = () if target is None else tuple(target)
    n_out = 1 + len(given)

    def kernel(side_ref, left_ref, *refs):
        weight_ref, outs = refs[-1 - n_out], refs[-n_out:]
        both = jnp.concatenate(
            [cut.pick(refs[i * each:i * each + n_first], refs[i * each + n_first]) for i in range(len(rights))], axis=0
        )
        step = (weight_rate * scale) * dot(left_ref[...], both, ((1,), (0,)))
        outs[0][...] = (weight_ref[:, cut.columns(side_ref)].astype(F32) - step).astype(BF16)
        if bias is not None:
            summed = jnp.sum(both.astype(F32), axis=0, keepdims=True)
            outs[1][...] = refs[each * len(rights)][...] - enc_bias_rate * summed

    operands = [left]
    for first, second in rights:
        operands += [*first, second]
    return run.call(
        kernel, cut.grid, (*operands, *given, *more),
        [IN_VMEM] + ([cut.first(count // n_first)] * n_first + [cut.second(count)]) * len(rights)
        + [cut.whole(1)] * len(given) + [UNTOUCHED] * len(more),
        [cut.whole(width)] + [cut.whole(1)] * len(given),
        [shape(width, latents)] + [shape(1, latents, dtype=F32)] * len(given),
        aliases={1 + len(operands) + len(given) + i: i for i in range(len(more))},
        use=[weight], vmem=14,
    )


def solution(mesh):
    n_rows, n_latent = mesh.shape["rows"], mesh.shape["latent"]
    row_bits = [1 << b for b in range(1, n_rows.bit_length() - 1)]
    latent_bits = [1 << b for b in range(n_latent.bit_length() - 1)]

    def beside(value):
        return flip(value, "rows", n_rows, 1)

    def across(run, value):
        for bit in row_bits[:-1]:
            value = added(run, value, flip(value, "rows", n_rows, bit))
        return value, flip(value, "rows", n_rows, row_bits[-1])

    def latent_terms(run, values):
        for bit in latent_bits[:-1]:
            received = [flip(value, "latent", n_latent, bit) for value in values]
            values = [added(run, *pair) for pair in zip(values, received)]
        return [(value, flip(value, "latent", n_latent, latent_bits[-1])) for value in values]

    def body(activations_in, gate_proj, up_proj, down_proj, enc_weight, enc_bias, dec_weight, dec_bias):
        width, local_latents = enc_weight.shape
        count = activations_in.shape[0] * activations_in.shape[1]
        enc_scale = (width * n_rows) ** -0.5
        dec_scale = (local_latents * n_latent) ** -0.5
        row = lax.axis_index("rows")
        core = row % 2
        own = core.astype(jnp.int32).reshape(1)

        parts = 2
        run = Order(own)
        pieces, (bias, out_bias) = token_parts(
            run, activations_in.reshape(count, activations_in.shape[2]).T, parts,
            (enc_bias.reshape(1, local_latents), dec_bias.reshape(1, width)),
        )
        if n_rows == n_latent:
            turn = [(a * n_rows + b, b * n_rows + a) for a in range(n_latent) for b in range(n_rows)]
            pieces = [lax.ppermute(piece, ("latent", "rows"), turn) for piece in pieces]
        else:
            pieces = [lax.all_gather(piece, "latent", axis=1, tiled=True) for piece in pieces]
            pieces = [lax.dynamic_slice_in_dim(piece, row * width, width, 1) for piece in pieces]

        cuts = cuts_of(local_latents // 2, (1, 1, 2))
        n_cuts = len(cuts)
        hidden = gate_proj.shape[1]
        run.keep(gate=gate_proj, up=up_proj, down=down_proj.T)
        run.keep(enc=enc_weight)
        chips = []
        for piece in pieces:
            received = beside(gate_or_up(run, False, piece, hidden))
            chips.append(across(run, gate_or_up(run, True, piece, hidden, received)))
        run.drop("gate", "up")
        layer_parts = []
        for mine, theirs in chips:
            half_term = added(run, mine, theirs, F32)
            layer_parts.append(layer_output(run, half_term, beside(half_term), width))
        run.drop("down")
        layer_terms = latent_terms(run, layer_parts)

        sums = [[None] * n_cuts for _ in range(parts)]
        backs = [[None] * n_cuts for _ in range(parts)]

        def project_all(tokens, weight, which, totals):
            held = None
            for i in [*which, None]:
                if i is not None:
                    for_other, mine = project(run, cuts[i], tokens, weight)
                    now = (i, mine, [beside(part) for part in for_other])
                if held is not None:
                    totals[held[0]] = across(run, added_parts(run, *held[1:]))
                held = now

        latents_own = [[None] * n_cuts for _ in range(parts)]
        latents_other = [[None] * n_cuts for _ in range(parts)]
        partials = [None] * parts

        def open_latents(part, i):
            latents_own[part][i], sent = latents_of(run, cuts[i], *sums[part][i], bias, enc_scale)
            latents_other[part][i] = [beside(piece) for piece in sent]

        def add_decoded(part, i):
            partials[part] = decode(
                run, cuts[i], latents_other[part][i], latents_own[part][i], "dec", width, partials[part], i == n_cuts - 1
            )

        def residual_of(part):
            return residual_grad(run, *latent_terms(run, [partials[part]])[0], out_bias, features[part], dec_scale)

        grads_own = [[None] * n_cuts for _ in range(parts)]
        grads_other = [[None] * n_cuts for _ in range(parts)]

        def open_grad(part, i):
            grads_own[part][i], sent = latent_grad(
                run, cuts[i], *sums[part][i], bias, *backs[part][i], enc_scale, dec_scale
            )
            grads_other[part][i] = [beside(piece) for piece in sent]

        early, late = [*range(n_cuts - 1)], n_cuts - 1
        features = [added(run, *layer_terms[0])]
        project_all(features[0], "enc", [*early, late], sums[0])
        features.append(added(run, *layer_terms[1]))
        waiting = []
        for i in [*early, late]:
            for_other, mine = project(run, cuts[i], features[1], "enc")
            waiting.append((mine, [beside(piece) for piece in for_other]))
        run.drop("enc")

        def send_second(i):
            sums[1][i] = across(run, added_parts(run, *waiting[i]))

        run.keep(dec=dec_weight.T)
        for i in early:
            open_latents(0, i)
            if i:
                add_decoded(0, i - 1)
                send_second(i - 1)
        if early:
            add_decoded(0, early[-1])
            send_second(early[-1])
        open_latents(0, late)
        send_second(late)
        add_decoded(0, late)
        for i in early:
            open_latents(1, i)
            add_decoded(1, i)
        residuals = [residual_of(0)]
        project_all(residuals[0], "dec", [*early, late], backs[0])
        open_latents(1, late)
        add_decoded(1, late)
        residuals.append(residual_of(1))
        if early:
            open_grad(0, 0)
        last_order = [late, *early]
        project_all(residuals[1], "dec", last_order, backs[1])

        residual_t = turned(run, residuals)
        dec_new = None
        for i in [*early, late]:
            if i:
                open_grad(0, i)
            rights = [(latents_other[part][i], latents_own[part][i]) for part in range(parts)]
            dec_new = update(
                run, cuts[i], residual_t, rights, "dec", dec_scale, dec_new, local_latents
            )
        if not early:
            open_grad(0, late)
        out_bias_new = update_bias(run, out_bias, residuals)

        run.drop("dec")
        run.keep(enc=enc_weight)
        features_t = turned(run, features)
        enc_new = None
        for i in last_order:
            open_grad(1, i)
            rights = [(grads_other[part][i], grads_own[part][i]) for part in range(parts)]
            enc_new = update(run, cuts[i], features_t, rights, "enc", enc_scale, enc_new, local_latents, bias)
        enc_new, bias_new = enc_new
        return enc_new, bias_new.reshape(local_latents), dec_new[0].T, out_bias_new

    return jax.shard_map(
        body,
        mesh=mesh,
        in_specs=(
            P("groups", None, "latent"),
            P("rows", "latent"),
            P("rows", "latent"),
            P("latent", "rows"),
            P(("groups", "rows"), "latent"),
            P(("groups", "latent")),
            P(("groups", "latent"), "rows"),
            P(("groups", "rows")),
        ),
        out_specs=(
            P(("groups", "rows"), "latent"),
            P(("groups", "latent")),
            P(("groups", "latent"), "rows"),
            P(("groups", "rows")),
        ),
        check_vma=False,
    )
```

```python
import math

import jax
import jax.numpy as jnp
from jax import lax
from jax.experimental import pallas as pl
from jax.experimental.pallas import tpu as pltpu
from jax.sharding import PartitionSpec as P

sparsity_cost = 0.1
sharpness = 8.0
weight_rate = 2.0
enc_bias_rate = 0.01
dec_bias_rate = 0.002

BF16, F32 = jnp.bfloat16, jnp.float32
MIB = 2 ** 20
IN_VMEM = pl.BlockSpec(memory_space=pltpu.VMEM)
UNTOUCHED = pl.BlockSpec(memory_space=pl.ANY)


def dot(a, b, over):
    return lax.dot_general(a, b, (over, ((), ())), preferred_element_type=F32)


def flip(value, axis, size, bit):
    return lax.ppermute(value, axis, [(i, i ^ bit) for i in range(size)])


SENT_PARTS = 2


def stacked(refs):
    return jnp.concatenate([ref[...] for ref in refs], axis=0)


def spread(value, refs):
    rows = refs[0].shape[0]
    for i, ref in enumerate(refs):
        ref[...] = value[i * rows:(i + 1) * rows]


class Cut:
    def __init__(self, half, start, width):
        self.half, self.start, self.width = half, start, width
        self.step = math.gcd(math.gcd(half, start), math.gcd(width, 4096))
        while self.step > 2048:
            self.step //= 2
        self.steps = width // self.step
        self.grid = 2 * self.steps

    def first(self, rows):
        return pl.BlockSpec((rows, self.step), lambda j, side: (0, jnp.minimum(j, self.steps - 1)))

    def second(self, rows):
        return pl.BlockSpec((rows, self.step), lambda j, side: (0, jnp.maximum(j - self.steps, 0)))

    def place(self, j, side):
        late = jnp.where(j < self.steps, 0, 1)
        half = jnp.where(j < self.steps, 1 - side[0], side[0])
        return (half * self.half + self.start) // self.step + j - late * self.steps

    def whole(self, rows):
        return pl.BlockSpec((rows, self.step), lambda j, side: (0, self.place(j, side)))

    def columns(self):
        return pl.ds(pl.multiple_of(pl.program_id(0) * self.step, self.step), self.step)

    def pick(self, first_refs, second_ref):
        return jnp.where(pl.program_id(0) < self.steps, stacked(first_refs), second_ref[...])


def cuts_of(half, shares):
    unit = half // sum(shares)
    if unit * sum(shares) != half or unit % 128:
        return [Cut(half, 0, half)]
    cuts, start = [], 0
    for share in shares:
        cuts.append(Cut(half, start, share * unit))
        start += share * unit
    return cuts


def shape(*dims, dtype=BF16):
    return jax.ShapeDtypeStruct(dims, dtype)


class Order:
    def __init__(self, side):
        self.side = side
        self.thread = jnp.zeros((8, 128), F32)
        self.kept = {}

    def call(self, kernel, grid, operands, in_specs, out_specs, out_shape, use=(), aliases=None, vmem=6, scratch=(),
             bring=None):
        names, bring = list(self.kept), bring or {}
        n_in, n_out, n_kept, n_new = len(operands), len(out_shape), len(names), len(bring)
        cuts = [cut for _, cut in bring.values()]

        def within(side_ref, *refs):
            ins, refs = refs[:n_in], refs[n_in:]
            weights, refs = dict(zip(names, refs[:n_kept])), refs[n_kept + 1:]
            sources, refs = refs[:n_new], refs[n_new:]
            outs, refs = refs[:n_out], refs[n_out + n_kept + 1:]
            targets, refs = refs[:n_new], refs[n_new:]

            def copies():
                made = []
                for source, target, cut in zip(sources, targets, cuts):
                    count = math.gcd(source.shape[0] // 16, 4)
                    rows = source.shape[0] // count
                    for half in range(1 if cut is None else 2):
                        for i in range(count):
                            start, end = source.at[pl.ds(i * rows, rows)], target.at[pl.ds(i * rows, rows)]
                            if cut is not None:
                                first = pl.multiple_of(cut.place(half * cut.steps, side_ref) * cut.step, cut.step)
                                start = source.at[pl.ds(i * rows, rows), pl.ds(first, cut.width)]
                                end = target.at[pl.ds(i * rows, rows), pl.ds(half * cut.width, cut.width)]
                            made.append(pltpu.make_async_copy(start, end, refs[-1].at[len(made)]))
                return made

            step = pl.program_id(0)

            @pl.when(step == 0)
            def _():
                for copy in copies():
                    copy.start()

            kernel(side_ref, *ins, *[weights[name] for name in use], *outs, *(refs[:-1] if bring else refs))

            @pl.when(step == grid - 1)
            def _():
                for copy in copies():
                    copy.wait()

        kept = [pltpu.with_memory_space_constraint(self.kept[name], pltpu.VMEM) for name in names]
        new = [pltpu.with_memory_space_constraint(weight, pltpu.HBM) for weight, _ in bring.values()]
        new_out = [
            pltpu.VMEM(weight.shape if cut is None else (weight.shape[0], 2 * cut.width), weight.dtype)
            for weight, cut in bring.values()
        ]
        joined = dict(aliases or {})
        joined.update({1 + n_in + i: n_out + i for i in range(n_kept + 1)})
        results = pl.pallas_call(
            within,
            grid_spec=pltpu.PrefetchScalarGridSpec(
                num_scalar_prefetch=1,
                grid=(grid,),
                in_specs=in_specs + [IN_VMEM] * n_kept + [UNTOUCHED] + [pl.BlockSpec(memory_space=pltpu.HBM)] * n_new,
                out_specs=out_specs + [IN_VMEM] * n_kept + [UNTOUCHED] + [IN_VMEM] * n_new,
                scratch_shapes=list(scratch) + ([pltpu.SemaphoreType.DMA((8 * n_new,))] if bring else []),
            ),
            out_shape=out_shape
            + [pltpu.VMEM(k.shape, k.dtype) for k in kept]
            + [shape(8, 128, dtype=F32)]
            + new_out,
            input_output_aliases=joined,
            compiler_params=pltpu.CompilerParams(vmem_limit_bytes=vmem * MIB),
            cost_estimate=pl.CostEstimate(flops=1, bytes_accessed=1, transcendentals=0),
        )(self.side, *operands, *kept, self.thread, *new)
        self.kept = dict(zip(names, results[n_out:]))
        self.thread = results[n_out + n_kept]
        self.kept.update(zip(bring, results[n_out + n_kept + 1:]))
        return list(results[:n_out])

    def keep(self, **weights):
        self.bring({name: (weight, None) for name, weight in weights.items()})

    def bring(self, new):
        self.call(lambda *refs: None, 1, (), [], [], [], vmem=1, bring=new)

    def drop(self, *names):
        for name in names:
            del self.kept[name]


def project(run, cut, tokens, weight, bring=None):
    count, width = tokens.shape

    def kernel(side_ref, tokens_ref, weight_ref, *refs):
        product = dot(tokens_ref[...], weight_ref[:, cut.columns()], ((1,), (0,))).astype(BF16)
        late = pl.program_id(0) >= cut.steps

        @pl.when(jnp.logical_not(late))
        def _():
            spread(product, refs[:-1])

        @pl.when(late)
        def _():
            refs[-1][...] = product

    each = count // SENT_PARTS
    *for_other, mine = run.call(
        kernel, cut.grid, (tokens,), [IN_VMEM], [cut.first(each)] * SENT_PARTS + [cut.second(count)],
        [shape(each, cut.width)] * SENT_PARTS + [shape(count, cut.width)], use=[weight], bring=bring,
    )
    return for_other, mine


def added(run, mine, received, dtype=BF16):
    def kernel(side_ref, mine_ref, received_ref, out_ref):
        out_ref[...] = (mine_ref[...].astype(F32) + received_ref[...].astype(F32)).astype(dtype)

    return run.call(
        kernel, 1, (mine, received), [IN_VMEM] * 2, [IN_VMEM], [shape(*mine.shape, dtype=dtype)],
    )[0]


def added_parts(run, pairs):
    count, width = pairs[0][0].shape[0], sum(mine.shape[1] for mine, _ in pairs)

    def kernel(side_ref, *refs):
        *refs, out_ref = refs
        first = 0
        for mine, received in pairs:
            (mine_ref, *received_refs), refs = refs[:1 + len(received)], refs[1 + len(received):]
            total = mine_ref[...].astype(F32) + stacked(received_refs).astype(F32)
            out_ref[:, first:first + mine.shape[1]] = total.astype(BF16)
            first += mine.shape[1]

    operands = [ref for mine, received in pairs for ref in (mine, *received)]
    return run.call(kernel, 1, operands, [IN_VMEM] * len(operands), [IN_VMEM], [shape(count, width)])[0]


def token_part(run, activations_t, part, parts):
    width, count = activations_t.shape
    each = count // parts

    def kernel(side_ref, activations_ref, out_ref):
        out_ref[...] = activations_ref[...].T[part * each:(part + 1) * each]

    return run.call(kernel, 1, (activations_t,), [IN_VMEM], [IN_VMEM], [shape(each, width)])[0]


def handed_on(run, arrays):
    return run.call(
        lambda *refs: None, 1, arrays, [UNTOUCHED] * len(arrays), [UNTOUCHED] * len(arrays),
        [shape(*a.shape, dtype=a.dtype) for a in arrays], aliases={1 + i: i for i in range(len(arrays))},
    )


def turned(run, parts):
    count, width = parts[0].shape

    def kernel(side_ref, first_ref, second_ref, out_ref):
        out_ref[...] = jnp.concatenate([first_ref[...], second_ref[...]], axis=0).T

    return run.call(
        kernel, 1, tuple(parts), [IN_VMEM] * 2, [IN_VMEM], [shape(width, 2 * count)]
    )[0]


def residual_grad(run, mine, received, bias, features, dec_scale):
    def kernel(side_ref, mine_ref, received_ref, bias_ref, features_ref, out_ref):
        rebuilt = dec_scale * (mine_ref[...].astype(F32) + received_ref[...].astype(F32)) + bias_ref[...]
        out_ref[...] = (2.0 * (rebuilt - features_ref[...].astype(F32))).astype(BF16)

    return run.call(
        kernel, 1, (mine, received, bias, features), [IN_VMEM] * 4, [IN_VMEM], [shape(*features.shape)],
    )[0]


def update_bias(run, bias, parts):
    def kernel(side_ref, bias_ref, first_ref, second_ref, out_ref):
        both = jnp.concatenate([first_ref[...], second_ref[...]], axis=0).astype(F32)
        out_ref[...] = (bias_ref[...] - dec_bias_rate * jnp.sum(both, axis=0, keepdims=True)).reshape(out_ref.shape)

    return run.call(
        kernel, 1, (bias,) + tuple(parts), [IN_VMEM] * 3, [IN_VMEM], [shape(bias.shape[1], dtype=F32)],
    )[0]


def gate_or_up(run, own, tokens, hidden, received=()):
    count = tokens.shape[0]
    n_out = 1 if own else SENT_PARTS

    def kernel(side_ref, tokens_ref, *refs):
        gate_ref, up_ref, *out_refs = refs[len(received):]
        for value, weight_ref in enumerate((gate_ref, up_ref) if own else (up_ref, gate_ref)):
            @pl.when(side_ref[0] == value)
            def _():
                total = dot(tokens_ref[...], weight_ref[...], ((1,), (0,)))
                if received:
                    total = total + stacked(refs[:len(received)]).astype(F32)
                spread(total.astype(BF16), out_refs)

    return run.call(
        kernel, 1, (tokens, *received), [IN_VMEM] * (1 + len(received)), [IN_VMEM] * n_out,
        [shape(count // n_out, hidden)] * n_out, use=["gate", "up"],
    )


def summed_term(run, mine, received):
    count, hidden = mine.shape

    def kernel(side_ref, mine_ref, received_ref, out_ref, *sent_refs):
        total = mine_ref[...].astype(F32) + received_ref[...].astype(F32)
        out_ref[...] = total
        spread(total, sent_refs)

    total, *sent = run.call(
        kernel, 1, (mine, received), [IN_VMEM] * 2, [IN_VMEM] * (1 + SENT_PARTS),
        [shape(count, hidden, dtype=F32)] + [shape(count // SENT_PARTS, hidden, dtype=F32)] * SENT_PARTS,
    )
    return total, sent


def layer_output(run, own_term, other_parts, width):
    count, hidden = own_term.shape

    def kernel(side_ref, own_ref, *refs):
        *other_refs, down_ref, out_ref = refs
        own_value, other_value = own_ref[...], stacked(other_refs)
        for value, (gate, up) in enumerate(((own_value, other_value), (other_value, own_value))):
            @pl.when(side_ref[0] == value)
            def _():
                hidden = (jax.nn.gelu(gate, approximate=True) * up).astype(BF16)
                out_ref[...] = dot(hidden, down_ref[...], ((1,), (1,))).astype(BF16)

    return run.call(
        kernel, 1, (own_term, *other_parts), [IN_VMEM] * (1 + len(other_parts)), [IN_VMEM], [shape(count, width)],
        use=["down"],
    )[0]


def pre_of(mine, other, bias, enc_scale):
    return enc_scale * (mine.astype(F32) + other.astype(F32)) + bias


def over_own(cut):
    def local(rows, first=0):
        return pl.BlockSpec((rows, cut.step), lambda j, side: (0, first // cut.step + j))

    def whole(rows):
        return pl.BlockSpec((rows, cut.step), lambda j, side: (0, cut.place(j + cut.steps, side)))

    return local, whole


def latents_of(run, cut, mine, other, first, bias, enc_scale):
    count = mine.shape[0]
    local, whole = over_own(cut)

    def kernel(side_ref, mine_ref, other_ref, bias_ref, latents_ref, *sent_refs):
        scaled = sharpness * pre_of(mine_ref[...], other_ref[...], bias_ref[...], enc_scale)
        soft = jnp.maximum(scaled, 0.0) + jnp.log1p(jnp.exp(-jnp.abs(scaled)))
        latents = (soft * (1.0 / sharpness)).astype(BF16)
        latents_ref[...] = latents
        spread(latents, sent_refs)

    each = count // SENT_PARTS
    latents, *sent = run.call(
        kernel, cut.steps, (mine, other, bias), [local(count, first), local(count, first), whole(1)],
        [local(count)] + [local(each)] * SENT_PARTS,
        [shape(count, cut.width)] + [shape(each, cut.width)] * SENT_PARTS,
    )
    return latents, sent


def decode(run, cut, latents_other, latents_own, weight, width, partial, last, bring=None):
    count = latents_own.shape[0]

    n_first = len(latents_other)

    def kernel(side_ref, *refs):
        first_refs, second_ref = refs[:n_first], refs[n_first]
        weight_ref, sum_ref, total = refs[-3:]

        @pl.when(pl.program_id(0) == 0)
        def _():
            total[...] = jnp.zeros_like(total) if partial is None else refs[n_first + 1][...]

        total[...] += dot(
            cut.pick(first_refs, second_ref), weight_ref[:, cut.columns()], ((1,), (1,))
        )

        @pl.when(pl.program_id(0) == cut.grid - 1)
        def _():
            sum_ref[...] = total[...].astype(sum_ref.dtype)

    more = () if partial is None else (partial,)
    return run.call(
        kernel, cut.grid, (*latents_other, latents_own) + more,
        [cut.first(count // n_first)] * n_first + [cut.second(count)] + [IN_VMEM] * len(more),
        [pl.BlockSpec((count, width), lambda j, side: (0, 0))],
        [shape(count, width, dtype=BF16 if last else F32)],
        use=[weight], scratch=[pltpu.VMEM((count, width), F32)], bring=bring,
    )[0]


def latent_grad(run, cut, mine, other, first, bias, back, back_other, back_first, enc_scale, dec_scale, sent_parts):
    count = mine.shape[0]
    local, whole = over_own(cut)

    def kernel(side_ref, mine_ref, other_ref, bias_ref, back_ref, back_other_ref, grad_ref, *sent_refs):
        scaled = sharpness * pre_of(mine_ref[...], other_ref[...], bias_ref[...], enc_scale)
        total = back_ref[...].astype(F32) + back_other_ref[...].astype(F32)
        grad = (jax.nn.sigmoid(scaled) * (dec_scale * total + sparsity_cost)).astype(BF16)
        grad_ref[...] = grad
        spread(grad, sent_refs)

    each = count // sent_parts
    grad, *sent = run.call(
        kernel, cut.steps, (mine, other, bias, back, back_other),
        [local(count, first), local(count, first), whole(1)] + [local(count, back_first)] * 2,
        [local(count)] + [local(each)] * sent_parts,
        [shape(count, cut.width)] + [shape(each, cut.width)] * sent_parts,
    )
    return grad, sent


def update(run, cut, left, rights, weight, scale, target, latents, bias=None, bring=None):
    width = left.shape[0]
    count = rights[0][1].shape[0]
    given = () if bias is None else (bias,)
    more = () if target is None else tuple(target)
    n_out = 1 + len(given)

    def kernel(side_ref, left_ref, *refs):
        weight_ref, outs = refs[-1 - n_out], refs[-n_out:]
        picked, used = [], 0
        for first, _ in rights:
            picked.append(cut.pick(refs[used:used + len(first)], refs[used + len(first)]))
            used += len(first) + 1
        both = jnp.concatenate(picked, axis=0)
        step = (weight_rate * scale) * dot(left_ref[...], both, ((1,), (0,)))
        outs[0][...] = (weight_ref[:, cut.columns()].astype(F32) - step).astype(BF16)
        if bias is not None:
            summed = jnp.sum(both.astype(F32), axis=0, keepdims=True)
            outs[1][...] = refs[used][...] - enc_bias_rate * summed

    operands, specs = [left], [IN_VMEM]
    for first, second in rights:
        operands += [*first, second]
        specs += [cut.first(count // len(first))] * len(first) + [cut.second(count)]
    return run.call(
        kernel, cut.grid, (*operands, *given, *more),
        specs + [cut.whole(1)] * len(given) + [UNTOUCHED] * len(more),
        [cut.whole(width)] + [cut.whole(1)] * len(given),
        [shape(width, latents)] + [shape(1, latents, dtype=F32)] * len(given),
        aliases={1 + len(operands) + len(given) + i: i for i in range(len(more))},
        use=[weight], vmem=14, bring=bring,
    )


def solution(mesh):
    n_rows, n_latent = mesh.shape["rows"], mesh.shape["latent"]
    row_bits = [1 << b for b in range(1, n_rows.bit_length() - 1)]
    latent_bits = [1 << b for b in range(n_latent.bit_length() - 1)]

    def beside(value):
        return flip(value, "rows", n_rows, 1)

    def across(run, value):
        for bit in row_bits[:-1]:
            value = added(run, value, flip(value, "rows", n_rows, bit))
        return value, flip(value, "rows", n_rows, row_bits[-1])

    def body(activations_in, gate_proj, up_proj, down_proj, enc_weight, enc_bias, dec_weight, dec_bias):
        width, local_latents = enc_weight.shape
        count = activations_in.shape[0] * activations_in.shape[1]
        enc_scale = (width * n_rows) ** -0.5
        dec_scale = (local_latents * n_latent) ** -0.5
        row = lax.axis_index("rows")
        core = row % 2
        own = core.astype(jnp.int32).reshape(1)

        parts = 2
        run = Order(own)
        turn = [(a * n_rows + b, b * n_rows + a) for a in range(n_latent) for b in range(n_rows)]
        activations_t = activations_in.reshape(count, activations_in.shape[2]).T

        def own_rows(part):
            piece = token_part(run, activations_t, part, parts)
            if n_rows == n_latent:
                return lax.ppermute(piece, ("latent", "rows"), turn)
            piece = lax.all_gather(piece, "latent", axis=1, tiled=True)
            return lax.dynamic_slice_in_dim(piece, row * width, width, 1)

        pieces = [own_rows(0)]
        bias, out_bias = handed_on(run, (enc_bias.reshape(1, local_latents), dec_bias.reshape(1, width)))
        cuts = cuts_of(local_latents // 2, (1, 1, 2))
        n_cuts = len(cuts)
        hidden = gate_proj.shape[1]
        early, late = [*range(n_cuts - 1)], n_cuts - 1
        last_order = [late, *early]
        dec_t = dec_weight.T

        def piece_of(name, i):
            return {(name, i): (enc_weight if name == "enc" else dec_t, cuts[i])}

        run.keep(gate=gate_proj, up=up_proj, down=down_proj.T)
        for i in range(n_cuts):
            run.bring(piece_of("enc", i))
        pieces.append(own_rows(1))
        chips = []
        for piece in pieces:
            received = [beside(part) for part in gate_or_up(run, False, piece, hidden)]
            chips.append(across(run, *gate_or_up(run, True, piece, hidden, received)))
        run.drop("gate", "up")

        def latent_terms(value, between):
            between = list(between)
            for bit in latent_bits:
                received = flip(value, "latent", n_latent, bit)
                if between:
                    between.pop(0)()
                if bit != latent_bits[-1]:
                    value = added(run, value, received)
            for rest in between:
                rest()
            return value, received

        layer_sums, layer_parts = [None] * parts, [None] * parts

        def open_layer(part):
            term, sent = summed_term(run, *chips[part])
            layer_sums[part] = (term, [beside(piece) for piece in sent])

        def close_layer(part):
            layer_parts[part] = layer_output(run, *layer_sums[part], width)

        open_layer(0)
        close_layer(0)
        def second_layer():
            open_layer(1)
            close_layer(1)

        layer_terms = latent_terms(layer_parts[0], [lambda: None, second_layer])
        run.drop("down")

        sums = [[None] * n_cuts for _ in range(parts)]
        backs = [[None] * n_cuts for _ in range(parts)]

        def project_start(part, i, tokens, weight, bring=None):
            for_other, mine = project(run, cuts[i], tokens, (weight, i), bring)
            return mine, [beside(piece) for piece in for_other]

        def project_end(part, which, totals):
            mine, theirs = across(run, added_parts(run, [held[part][i] for i in which]))
            first = 0
            for i in which:
                totals[part][i] = (mine, theirs, first)
                first += cuts[i].width

        latents_own = [[None] * n_cuts for _ in range(parts)]
        latents_other = [[None] * n_cuts for _ in range(parts)]
        partials = [None] * parts

        def open_latents(part, i):
            latents_own[part][i], sent = latents_of(run, cuts[i], *sums[part][i], bias, enc_scale)
            latents_other[part][i] = [beside(piece) for piece in sent]

        def add_decoded(part, i, bring=None):
            partials[part] = decode(
                run, cuts[i], latents_other[part][i], latents_own[part][i], ("dec", i), width, partials[part],
                i == n_cuts - 1, bring,
            )

        grads_own = [[None] * n_cuts for _ in range(parts)]
        grads_other = [[None] * n_cuts for _ in range(parts)]

        def open_grad(part, i):
            grads_own[part][i], sent = latent_grad(
                run, cuts[i], *sums[part][i], bias, *backs[part][i], enc_scale, dec_scale,
                2 if part else 2,
            )
            grads_other[part][i] = [beside(piece) for piece in sent]

        features, held = [added(run, *layer_terms)], [[None] * n_cuts for _ in range(parts)]

        def encode_first():
            for i in early:
                held[0][i] = project_start(0, i, features[0], "enc")
            if early:
                project_end(0, early, sums)
            held[0][late] = project_start(0, late, features[0], "enc", piece_of("dec", 0) if early else None)

        layer_terms = latent_terms(layer_parts[1], [lambda: None, encode_first])
        features.append(added(run, *layer_terms))
        project_end(0, [late], sums)
        for i in range(n_cuts):
            bring = piece_of("dec", i + 1) if i + 1 < late else piece_of("dec", late) if i == late else None
            held[1][i] = project_start(1, i, features[1], "enc", bring)
            run.drop(("enc", i))

        for i in early:
            open_latents(0, i)
        for i in early:
            if i == min(1, late - 1):
                project_end(1, early, sums)
            add_decoded(0, i)
        open_latents(0, late)
        project_end(1, [late], sums)
        add_decoded(0, late)

        def residual_of(part, between):
            terms = latent_terms(partials[part], between)
            return residual_grad(run, *terms, out_bias, features[part], dec_scale)

        residuals = [residual_of(0, [lambda i=i: open_latents(1, i) for i in early])]
        for i in range(n_cuts):
            held[0][i] = project_start(0, i, residuals[0], "dec")
        project_end(0, range(n_cuts), backs)
        open_latents(1, late)
        for i in range(n_cuts):
            add_decoded(1, i)
        residuals.append(residual_of(1, []))

        dec_new = enc_new = residual_t = features_t = None

        def write_dec(k):
            i = last_order[k]
            rights = [(latents_other[part][i], latents_own[part][i]) for part in range(parts)]
            new = update(
                run, cuts[i], residual_t, rights, ("dec", i), dec_scale, dec_new, local_latents,
                bring=piece_of("enc", last_order[k - 1]) if k else None,
            )
            run.drop(("dec", i))
            return new

        def write_enc(k):
            i = last_order[k]
            rights = [(grads_other[part][i], grads_own[part][i]) for part in range(parts)]
            new = update(
                run, cuts[i], features_t, rights, ("enc", i), enc_scale, enc_new, local_latents, bias,
                bring=piece_of("enc", last_order[-1]) if k == n_cuts - 2 else None,
            )
            run.drop(("enc", i))
            return new

        for i in last_order:
            held[1][i] = project_start(1, i, residuals[1], "dec")
        project_end(1, [late], backs)
        if early:
            project_end(1, early, backs)
        residual_t = turned(run, residuals)
        features_t = turned(run, features)
        for k in range(n_cuts):
            dec_new = write_dec(k)
            if k == 0:
                for i in last_order:
                    open_grad(0, i)
        out_bias_new = update_bias(run, out_bias, residuals)
        if n_cuts == 1:
            run.bring(piece_of("enc", late))
        open_grad(1, late)
        for k in range(n_cuts):
            if k == 1:
                for i in early:
                    open_grad(1, i)
            enc_new = write_enc(k)
        enc_new, bias_new = enc_new
        return enc_new, bias_new.reshape(local_latents), dec_new[0].T, out_bias_new

    return jax.shard_map(
        body,
        mesh=mesh,
        in_specs=(
            P("groups", None, "latent"),
            P("rows", "latent"),
            P("rows", "latent"),
            P("latent", "rows"),
            P(("groups", "rows"), "latent"),
            P(("groups", "latent")),
            P(("groups", "latent"), "rows"),
            P(("groups", "rows")),
        ),
        out_specs=(
            P(("groups", "rows"), "latent"),
            P(("groups", "latent")),
            P(("groups", "latent"), "rows"),
            P(("groups", "rows")),
        ),
        check_vma=False,
    )
```

```python
import math

import jax
import jax.numpy as jnp
from jax import lax
from jax.experimental import pallas as pl
from jax.experimental.pallas import tpu as pltpu
from jax.sharding import PartitionSpec as P

sparsity_cost = 0.1
sharpness = 8.0
weight_rate = 2.0
enc_bias_rate = 0.01
dec_bias_rate = 0.002

BF16, F32 = jnp.bfloat16, jnp.float32
MIB = 2 ** 20
IN_VMEM = pl.BlockSpec(memory_space=pltpu.VMEM)
UNTOUCHED = pl.BlockSpec(memory_space=pl.ANY)


def dot(a, b, over):
    return lax.dot_general(a, b, (over, ((), ())), preferred_element_type=F32)


def flip(value, axis, size, bit):
    return lax.ppermute(value, axis, [(i, i ^ bit) for i in range(size)])


SENT_PARTS = 2


def stacked(refs):
    return jnp.concatenate([ref[...] for ref in refs], axis=0)


def spread(value, refs):
    rows = refs[0].shape[0]
    for i, ref in enumerate(refs):
        ref[...] = value[i * rows:(i + 1) * rows]


class Cut:
    def __init__(self, half, start, width):
        self.half, self.start, self.width = half, start, width
        self.step = math.gcd(math.gcd(half, start), math.gcd(width, 4096))
        while self.step > 2048:
            self.step //= 2
        self.steps = width // self.step
        self.grid = 2 * self.steps

    def first(self, rows):
        return pl.BlockSpec((rows, self.step), lambda j, side: (0, jnp.minimum(j, self.steps - 1)))

    def second(self, rows):
        return pl.BlockSpec((rows, self.step), lambda j, side: (0, jnp.maximum(j - self.steps, 0)))

    def place(self, j, side):
        late = jnp.where(j < self.steps, 0, 1)
        half = jnp.where(j < self.steps, 1 - side[0], side[0])
        return (half * self.half + self.start) // self.step + j - late * self.steps

    def whole(self, rows):
        return pl.BlockSpec((rows, self.step), lambda j, side: (0, self.place(j, side)))

    def columns(self):
        return pl.ds(pl.multiple_of(pl.program_id(0) * self.step, self.step), self.step)

    def pick(self, first_refs, second_ref):
        return jnp.where(pl.program_id(0) < self.steps, stacked(first_refs), second_ref[...])


def cuts_of(half, shares):
    unit = half // sum(shares)
    if unit * sum(shares) != half or unit % 128:
        return [Cut(half, 0, half)]
    cuts, start = [], 0
    for share in shares:
        cuts.append(Cut(half, start, share * unit))
        start += share * unit
    return cuts


def shape(*dims, dtype=BF16):
    return jax.ShapeDtypeStruct(dims, dtype)


class Order:
    def __init__(self, side):
        self.side = side
        self.thread = jnp.zeros((8, 128), F32)
        self.kept = {}

    def call(self, kernel, grid, operands, in_specs, out_specs, out_shape, use=(), aliases=None, vmem=6, scratch=(),
             bring=None):
        names, bring = list(self.kept), bring or {}
        n_in, n_out, n_kept, n_new = len(operands), len(out_shape), len(names), len(bring)
        cuts = [cut for _, cut in bring.values()]

        def within(side_ref, *refs):
            ins, refs = refs[:n_in], refs[n_in:]
            weights, refs = dict(zip(names, refs[:n_kept])), refs[n_kept + 1:]
            sources, refs = refs[:n_new], refs[n_new:]
            outs, refs = refs[:n_out], refs[n_out + n_kept + 1:]
            targets, refs = refs[:n_new], refs[n_new:]

            def copies():
                made = []
                for source, target, cut in zip(sources, targets, cuts):
                    count = math.gcd(source.shape[0] // 16, 4)
                    rows = source.shape[0] // count
                    for half in range(1 if cut is None else 2):
                        for i in range(count):
                            start, end = source.at[pl.ds(i * rows, rows)], target.at[pl.ds(i * rows, rows)]
                            if cut is not None:
                                first = pl.multiple_of(cut.place(half * cut.steps, side_ref) * cut.step, cut.step)
                                start = source.at[pl.ds(i * rows, rows), pl.ds(first, cut.width)]
                                end = target.at[pl.ds(i * rows, rows), pl.ds(half * cut.width, cut.width)]
                            made.append(pltpu.make_async_copy(start, end, refs[-1].at[len(made)]))
                return made

            step = pl.program_id(0)

            @pl.when(step == 0)
            def _():
                for copy in copies():
                    copy.start()

            kernel(side_ref, *ins, *[weights[name] for name in use], *outs, *(refs[:-1] if bring else refs))

            @pl.when(step == grid - 1)
            def _():
                for copy in copies():
                    copy.wait()

        kept = [pltpu.with_memory_space_constraint(self.kept[name], pltpu.VMEM) for name in names]
        new = [pltpu.with_memory_space_constraint(weight, pltpu.HBM) for weight, _ in bring.values()]
        new_out = [
            pltpu.VMEM(weight.shape if cut is None else (weight.shape[0], 2 * cut.width), weight.dtype)
            for weight, cut in bring.values()
        ]
        joined = dict(aliases or {})
        joined.update({1 + n_in + i: n_out + i for i in range(n_kept + 1)})
        results = pl.pallas_call(
            within,
            grid_spec=pltpu.PrefetchScalarGridSpec(
                num_scalar_prefetch=1,
                grid=(grid,),
                in_specs=in_specs + [IN_VMEM] * n_kept + [UNTOUCHED] + [pl.BlockSpec(memory_space=pltpu.HBM)] * n_new,
                out_specs=out_specs + [IN_VMEM] * n_kept + [UNTOUCHED] + [IN_VMEM] * n_new,
                scratch_shapes=list(scratch) + ([pltpu.SemaphoreType.DMA((8 * n_new,))] if bring else []),
            ),
            out_shape=out_shape
            + [pltpu.VMEM(k.shape, k.dtype) for k in kept]
            + [shape(8, 128, dtype=F32)]
            + new_out,
            input_output_aliases=joined,
            compiler_params=pltpu.CompilerParams(vmem_limit_bytes=vmem * MIB),
            cost_estimate=pl.CostEstimate(flops=1, bytes_accessed=1, transcendentals=0),
        )(self.side, *operands, *kept, self.thread, *new)
        self.kept = dict(zip(names, results[n_out:]))
        self.thread = results[n_out + n_kept]
        self.kept.update(zip(bring, results[n_out + n_kept + 1:]))
        return list(results[:n_out])

    def keep(self, **weights):
        self.bring({name: (weight, None) for name, weight in weights.items()})

    def bring(self, new):
        self.call(lambda *refs: None, 1, (), [], [], [], vmem=1, bring=new)

    def drop(self, *names):
        for name in names:
            del self.kept[name]


def project(run, cut, tokens, weight, sent_parts=SENT_PARTS, bring=None):
    count, width = tokens.shape

    def kernel(side_ref, tokens_ref, weight_ref, *refs):
        product = dot(tokens_ref[...], weight_ref[:, cut.columns()], ((1,), (0,))).astype(BF16)
        late = pl.program_id(0) >= cut.steps

        @pl.when(jnp.logical_not(late))
        def _():
            spread(product, refs[:-1])

        @pl.when(late)
        def _():
            refs[-1][...] = product

    each = count // sent_parts
    *for_other, mine = run.call(
        kernel, cut.grid, (tokens,), [IN_VMEM], [cut.first(each)] * sent_parts + [cut.second(count)],
        [shape(each, cut.width)] * sent_parts + [shape(count, cut.width)], use=[weight], bring=bring,
    )
    return for_other, mine


def added(run, mine, received, dtype=BF16):
    def kernel(side_ref, mine_ref, received_ref, out_ref):
        out_ref[...] = (mine_ref[...].astype(F32) + received_ref[...].astype(F32)).astype(dtype)

    return run.call(
        kernel, 1, (mine, received), [IN_VMEM] * 2, [IN_VMEM], [shape(*mine.shape, dtype=dtype)],
    )[0]


def added_parts(run, pairs):
    count, width = pairs[0][0].shape[0], sum(mine.shape[1] for mine, _ in pairs)

    def kernel(side_ref, *refs):
        *refs, out_ref = refs
        first = 0
        for mine, received in pairs:
            (mine_ref, *received_refs), refs = refs[:1 + len(received)], refs[1 + len(received):]
            total = mine_ref[...].astype(F32) + stacked(received_refs).astype(F32)
            out_ref[:, first:first + mine.shape[1]] = total.astype(BF16)
            first += mine.shape[1]

    operands = [ref for mine, received in pairs for ref in (mine, *received)]
    return run.call(kernel, 1, operands, [IN_VMEM] * len(operands), [IN_VMEM], [shape(count, width)])[0]


def token_part(run, activations_t, part, parts):
    width, count = activations_t.shape
    each = count // parts

    def kernel(side_ref, activations_ref, out_ref):
        out_ref[...] = activations_ref[...].T[part * each:(part + 1) * each]

    return run.call(kernel, 1, (activations_t,), [IN_VMEM], [IN_VMEM], [shape(each, width)])[0]


def handed_on(run, arrays):
    return run.call(
        lambda *refs: None, 1, arrays, [UNTOUCHED] * len(arrays), [UNTOUCHED] * len(arrays),
        [shape(*a.shape, dtype=a.dtype) for a in arrays], aliases={1 + i: i for i in range(len(arrays))},
    )


def turned(run, parts):
    count, width = parts[0].shape

    def kernel(side_ref, first_ref, second_ref, out_ref):
        out_ref[...] = jnp.concatenate([first_ref[...], second_ref[...]], axis=0).T

    return run.call(
        kernel, 1, tuple(parts), [IN_VMEM] * 2, [IN_VMEM], [shape(width, 2 * count)]
    )[0]


def residual_grad(run, mine, received, bias, features, dec_scale):
    def kernel(side_ref, mine_ref, received_ref, bias_ref, features_ref, out_ref):
        rebuilt = dec_scale * (mine_ref[...].astype(F32) + received_ref[...].astype(F32)) + bias_ref[...]
        out_ref[...] = (2.0 * (rebuilt - features_ref[...].astype(F32))).astype(BF16)

    return run.call(
        kernel, 1, (mine, received, bias, features), [IN_VMEM] * 4, [IN_VMEM], [shape(*features.shape)],
    )[0]


def update_bias(run, bias, parts):
    def kernel(side_ref, bias_ref, first_ref, second_ref, out_ref):
        both = jnp.concatenate([first_ref[...], second_ref[...]], axis=0).astype(F32)
        out_ref[...] = (bias_ref[...] - dec_bias_rate * jnp.sum(both, axis=0, keepdims=True)).reshape(out_ref.shape)

    return run.call(
        kernel, 1, (bias,) + tuple(parts), [IN_VMEM] * 3, [IN_VMEM], [shape(bias.shape[1], dtype=F32)],
    )[0]


def gate_or_up(run, own, tokens, hidden, received=()):
    count = tokens.shape[0]
    n_out = 1 if own else SENT_PARTS

    def kernel(side_ref, tokens_ref, *refs):
        gate_ref, up_ref, *out_refs = refs[len(received):]
        for value, weight_ref in enumerate((gate_ref, up_ref) if own else (up_ref, gate_ref)):
            @pl.when(side_ref[0] == value)
            def _():
                total = dot(tokens_ref[...], weight_ref[...], ((1,), (0,)))
                if received:
                    total = total + stacked(refs[:len(received)]).astype(F32)
                spread(total.astype(BF16), out_refs)

    return run.call(
        kernel, 1, (tokens, *received), [IN_VMEM] * (1 + len(received)), [IN_VMEM] * n_out,
        [shape(count // n_out, hidden)] * n_out, use=["gate", "up"],
    )


def summed_term(run, mine, received):
    count, hidden = mine.shape

    def kernel(side_ref, mine_ref, received_ref, out_ref, *sent_refs):
        total = mine_ref[...].astype(F32) + received_ref[...].astype(F32)
        out_ref[...] = total
        spread(total, sent_refs)

    total, *sent = run.call(
        kernel, 1, (mine, received), [IN_VMEM] * 2, [IN_VMEM] * (1 + SENT_PARTS),
        [shape(count, hidden, dtype=F32)] + [shape(count // SENT_PARTS, hidden, dtype=F32)] * SENT_PARTS,
    )
    return total, sent


def layer_output(run, own_term, other_parts, width):
    count, hidden = own_term.shape

    def kernel(side_ref, own_ref, *refs):
        *other_refs, down_ref, out_ref = refs
        own_value, other_value = own_ref[...], stacked(other_refs)
        for value, (gate, up) in enumerate(((own_value, other_value), (other_value, own_value))):
            @pl.when(side_ref[0] == value)
            def _():
                hidden = (jax.nn.gelu(gate, approximate=True) * up).astype(BF16)
                out_ref[...] = dot(hidden, down_ref[...], ((1,), (1,))).astype(BF16)

    return run.call(
        kernel, 1, (own_term, *other_parts), [IN_VMEM] * (1 + len(other_parts)), [IN_VMEM], [shape(count, width)],
        use=["down"],
    )[0]


def pre_of(mine, other, bias, enc_scale):
    return enc_scale * (mine.astype(F32) + other.astype(F32)) + bias


def over_own(cut):
    def local(rows, first=0):
        return pl.BlockSpec((rows, cut.step), lambda j, side: (0, first // cut.step + j))

    def whole(rows):
        return pl.BlockSpec((rows, cut.step), lambda j, side: (0, cut.place(j + cut.steps, side)))

    return local, whole


def latents_of(run, cut, mine, other, first, bias, enc_scale, sent_parts=SENT_PARTS):
    count = mine.shape[0]
    local, whole = over_own(cut)

    def kernel(side_ref, mine_ref, other_ref, bias_ref, latents_ref, *sent_refs):
        scaled = sharpness * pre_of(mine_ref[...], other_ref[...], bias_ref[...], enc_scale)
        soft = jnp.maximum(scaled, 0.0) + jnp.log1p(jnp.exp(-jnp.abs(scaled)))
        latents = (soft * (1.0 / sharpness)).astype(BF16)
        latents_ref[...] = latents
        spread(latents, sent_refs)

    each = count // sent_parts
    latents, *sent = run.call(
        kernel, cut.steps, (mine, other, bias), [local(count, first), local(count, first), whole(1)],
        [local(count)] + [local(each)] * sent_parts,
        [shape(count, cut.width)] + [shape(each, cut.width)] * sent_parts,
    )
    return latents, sent


def decode(run, cut, latents_other, latents_own, weight, width, partial, last, bring=None):
    count = latents_own.shape[0]

    n_first = len(latents_other)

    def kernel(side_ref, *refs):
        first_refs, second_ref = refs[:n_first], refs[n_first]
        weight_ref, sum_ref, total = refs[-3:]

        @pl.when(pl.program_id(0) == 0)
        def _():
            total[...] = jnp.zeros_like(total) if partial is None else refs[n_first + 1][...]

        total[...] += dot(
            cut.pick(first_refs, second_ref), weight_ref[:, cut.columns()], ((1,), (1,))
        )

        @pl.when(pl.program_id(0) == cut.grid - 1)
        def _():
            sum_ref[...] = total[...].astype(sum_ref.dtype)

    more = () if partial is None else (partial,)
    return run.call(
        kernel, cut.grid, (*latents_other, latents_own) + more,
        [cut.first(count // n_first)] * n_first + [cut.second(count)] + [IN_VMEM] * len(more),
        [pl.BlockSpec((count, width), lambda j, side: (0, 0))],
        [shape(count, width, dtype=BF16 if last else F32)],
        use=[weight], scratch=[pltpu.VMEM((count, width), F32)], bring=bring,
    )[0]


def latent_grad(run, cut, mine, other, first, bias, back, back_other, back_first, enc_scale, dec_scale, sent_parts):
    count = mine.shape[0]
    local, whole = over_own(cut)

    def kernel(side_ref, mine_ref, other_ref, bias_ref, back_ref, back_other_ref, grad_ref, *sent_refs):
        scaled = sharpness * pre_of(mine_ref[...], other_ref[...], bias_ref[...], enc_scale)
        total = back_ref[...].astype(F32) + back_other_ref[...].astype(F32)
        grad = (jax.nn.sigmoid(scaled) * (dec_scale * total + sparsity_cost)).astype(BF16)
        grad_ref[...] = grad
        spread(grad, sent_refs)

    each = count // sent_parts
    grad, *sent = run.call(
        kernel, cut.steps, (mine, other, bias, back, back_other),
        [local(count, first), local(count, first), whole(1)] + [local(count, back_first)] * 2,
        [local(count)] + [local(each)] * sent_parts,
        [shape(count, cut.width)] + [shape(each, cut.width)] * sent_parts,
    )
    return grad, sent


def update(run, cut, left, rights, weight, scale, target, latents, bias=None, bring=None):
    width = left.shape[0]
    count = rights[0][1].shape[0]
    given = () if bias is None else (bias,)
    more = () if target is None else tuple(target)
    n_out = 1 + len(given)

    def kernel(side_ref, left_ref, *refs):
        weight_ref, outs = refs[-1 - n_out], refs[-n_out:]
        picked, used = [], 0
        for first, _ in rights:
            picked.append(cut.pick(refs[used:used + len(first)], refs[used + len(first)]))
            used += len(first) + 1
        both = jnp.concatenate(picked, axis=0)
        step = (weight_rate * scale) * dot(left_ref[...], both, ((1,), (0,)))
        outs[0][...] = (weight_ref[:, cut.columns()].astype(F32) - step).astype(BF16)
        if bias is not None:
            summed = jnp.sum(both.astype(F32), axis=0, keepdims=True)
            outs[1][...] = refs[used][...] - enc_bias_rate * summed

    operands, specs = [left], [IN_VMEM]
    for first, second in rights:
        operands += [*first, second]
        specs += [cut.first(count // len(first))] * len(first) + [cut.second(count)]
    return run.call(
        kernel, cut.grid, (*operands, *given, *more),
        specs + [cut.whole(1)] * len(given) + [UNTOUCHED] * len(more),
        [cut.whole(width)] + [cut.whole(1)] * len(given),
        [shape(width, latents)] + [shape(1, latents, dtype=F32)] * len(given),
        aliases={1 + len(operands) + len(given) + i: i for i in range(len(more))},
        use=[weight], vmem=14, bring=bring,
    )


def solution(mesh):
    n_rows, n_latent = mesh.shape["rows"], mesh.shape["latent"]
    row_bits = [1 << b for b in range(1, n_rows.bit_length() - 1)]
    latent_bits = [1 << b for b in range(n_latent.bit_length() - 1)]

    def beside(value):
        return flip(value, "rows", n_rows, 1)

    def across(run, value):
        for bit in row_bits[:-1]:
            value = added(run, value, flip(value, "rows", n_rows, bit))
        return value, flip(value, "rows", n_rows, row_bits[-1])

    def body(activations_in, gate_proj, up_proj, down_proj, enc_weight, enc_bias, dec_weight, dec_bias):
        width, local_latents = enc_weight.shape
        count = activations_in.shape[0] * activations_in.shape[1]
        enc_scale = (width * n_rows) ** -0.5
        dec_scale = (local_latents * n_latent) ** -0.5
        row = lax.axis_index("rows")
        core = row % 2
        own = core.astype(jnp.int32).reshape(1)

        parts = 2
        run = Order(own)
        turn = [(a * n_rows + b, b * n_rows + a) for a in range(n_latent) for b in range(n_rows)]
        activations_t = activations_in.reshape(count, activations_in.shape[2]).T

        def own_rows(part):
            piece = token_part(run, activations_t, part, parts)
            if n_rows == n_latent:
                return lax.ppermute(piece, ("latent", "rows"), turn)
            piece = lax.all_gather(piece, "latent", axis=1, tiled=True)
            return lax.dynamic_slice_in_dim(piece, row * width, width, 1)

        pieces = [own_rows(0)]
        cuts = cuts_of(local_latents // 2, (1, 1, 2))
        n_cuts = len(cuts)
        hidden = gate_proj.shape[1]
        early, late = [*range(n_cuts - 1)], n_cuts - 1
        last_order = [late, *early]
        dec_t = dec_weight.T

        def piece_of(name, i):
            return {(name, i): (enc_weight if name == "enc" else dec_t, cuts[i])}

        run.keep(gate=gate_proj, up=up_proj, down=down_proj.T)
        pieces.append(own_rows(1))
        chips = []

        def start_layer(part):
            received = [beside(sent) for sent in gate_or_up(run, False, pieces[part], hidden)]
            chips.append(across(run, *gate_or_up(run, True, pieces[part], hidden, received)))

        start_layer(0)
        bias, out_bias = handed_on(run, (enc_bias.reshape(1, local_latents), dec_bias.reshape(1, width)))
        start_layer(1)
        run.drop("gate", "up")
        run.bring(piece_of("enc", 0))

        def latent_terms(value, between):
            between = list(between)
            for bit in latent_bits:
                received = flip(value, "latent", n_latent, bit)
                if between:
                    between.pop(0)()
                if bit != latent_bits[-1]:
                    value = added(run, value, received)
            for rest in between:
                rest()
            return value, received

        layer_sums, layer_parts = [None] * parts, [None] * parts

        def open_layer(part):
            term, sent = summed_term(run, *chips[part])
            layer_sums[part] = (term, [beside(piece) for piece in sent])

        def close_layer(part):
            layer_parts[part] = layer_output(run, *layer_sums[part], width)

        open_layer(0)
        close_layer(0)
        def second_layer():
            open_layer(1)
            close_layer(1)
            if n_cuts > 1:
                run.bring(piece_of("enc", late))

        def more_pieces():
            for i in early[1:]:
                run.bring(piece_of("enc", i))

        layer_terms = latent_terms(layer_parts[0], [more_pieces, second_layer])
        run.drop("down")

        sums = [[None] * n_cuts for _ in range(parts)]
        backs = [[None] * n_cuts for _ in range(parts)]

        def project_start(part, i, tokens, weight, bring=None, sent_parts=SENT_PARTS):
            for_other, mine = project(run, cuts[i], tokens, (weight, i), sent_parts, bring)
            return mine, [beside(piece) for piece in for_other]

        def project_end(part, which, totals):
            mine, theirs = across(run, added_parts(run, [held[part][i] for i in which]))
            first = 0
            for i in which:
                totals[part][i] = (mine, theirs, first)
                first += cuts[i].width

        latents_own = [[None] * n_cuts for _ in range(parts)]
        latents_other = [[None] * n_cuts for _ in range(parts)]
        partials = [None] * parts

        def open_latents(part, i):
            latents_own[part][i], sent = latents_of(
                run, cuts[i], *sums[part][i], bias, enc_scale, 2 * SENT_PARTS if part and i != late else SENT_PARTS
            )
            latents_other[part][i] = [beside(piece) for piece in sent]

        def add_decoded(part, i, bring=None):
            partials[part] = decode(
                run, cuts[i], latents_other[part][i], latents_own[part][i], ("dec", i), width, partials[part],
                i == n_cuts - 1, bring,
            )

        grads_own = [[None] * n_cuts for _ in range(parts)]
        grads_other = [[None] * n_cuts for _ in range(parts)]

        def open_grad(part, i):
            grads_own[part][i], sent = latent_grad(
                run, cuts[i], *sums[part][i], bias, *backs[part][i], enc_scale, dec_scale,
                2 if part else 2,
            )
            grads_other[part][i] = [beside(piece) for piece in sent]

        features, held = [added(run, *layer_terms)], [[None] * n_cuts for _ in range(parts)]

        def encode_first():
            for i in early:
                held[0][i] = project_start(0, i, features[0], "enc", sent_parts=2 * SENT_PARTS)

        layer_terms = latent_terms(layer_parts[1], [lambda: None, encode_first])
        features.append(added(run, *layer_terms))
        if early:
            project_end(0, early, sums)
        held[0][late] = project_start(0, late, features[0], "enc", piece_of("dec", 0) if early else None)
        project_end(0, [late], sums)
        for i in range(n_cuts):
            bring = piece_of("dec", i + 1) if i + 1 < late else None
            held[1][i] = project_start(1, i, features[1], "enc", bring)
            run.drop(("enc", i))

        for i in early:
            open_latents(0, i)
        for i in early:
            if i == min(1, late - 1):
                project_end(1, early, sums)
            add_decoded(0, i, piece_of("dec", late) if i == 0 else None)
        if not early:
            run.bring(piece_of("dec", late))
        open_latents(0, late)
        project_end(1, [late], sums)
        add_decoded(0, late)

        def residual_of(part, between):
            terms = latent_terms(partials[part], between)
            return residual_grad(run, *terms, out_bias, features[part], dec_scale)

        def open_second():
            for i in early:
                open_latents(1, i)

        def decode_second():
            for i in early:
                add_decoded(1, i)

        residuals = [residual_of(0, [open_second, decode_second])]
        for i in range(n_cuts):
            held[0][i] = project_start(0, i, residuals[0], "dec")
        project_end(0, range(n_cuts), backs)
        open_latents(1, late)
        add_decoded(1, late)
        residuals.append(residual_of(1, [lambda: run.bring(piece_of("enc", early[0])) if early else None]))

        dec_new = enc_new = residual_t = features_t = None

        def write_dec(k):
            i = last_order[k]
            rights = [(latents_other[part][i], latents_own[part][i]) for part in range(parts)]
            new = update(
                run, cuts[i], residual_t, rights, ("dec", i), dec_scale, dec_new, local_latents,
                bring=piece_of("enc", late) if k == min(n_cuts - 2, 1) else None,
            )
            run.drop(("dec", i))
            return new

        def write_enc(k):
            i = last_order[k]
            rights = [(grads_other[part][i], grads_own[part][i]) for part in range(parts)]
            new = update(
                run, cuts[i], features_t, rights, ("enc", i), enc_scale, enc_new, local_latents, bias,
                bring=piece_of("enc", early[k + 1]) if k + 1 < len(early) else None,
            )
            run.drop(("enc", i))
            return new

        residual_t = turned(run, residuals)
        features_t = turned(run, features)
        for i in last_order:
            held[1][i] = project_start(1, i, residuals[1], "dec")
        dec_new = write_dec(n_cuts - 1)
        project_end(1, [late], backs)
        if early:
            project_end(1, early, backs)
        for k in range(n_cuts - 1):
            dec_new = write_dec(k)
            if k == 0:
                for i in last_order:
                    open_grad(0, i)
        if n_cuts == 1:
            open_grad(0, late)
        out_bias_new = update_bias(run, out_bias, residuals)
        if n_cuts == 1:
            run.bring(piece_of("enc", late))
        open_grad(1, late)
        for k in range(n_cuts):
            if k == 1:
                for i in early:
                    open_grad(1, i)
            enc_new = write_enc(k)
        enc_new, bias_new = enc_new
        return enc_new, bias_new.reshape(local_latents), dec_new[0].T, out_bias_new

    return jax.shard_map(
        body,
        mesh=mesh,
        in_specs=(
            P("groups", None, "latent"),
            P("rows", "latent"),
            P("rows", "latent"),
            P("latent", "rows"),
            P(("groups", "rows"), "latent"),
            P(("groups", "latent")),
            P(("groups", "latent"), "rows"),
            P(("groups", "rows")),
        ),
        out_specs=(
            P(("groups", "rows"), "latent"),
            P(("groups", "latent")),
            P(("groups", "latent"), "rows"),
            P(("groups", "rows")),
        ),
        check_vma=False,
    )
```
